32 devices in a mesh: sweep: 2 (over y), dp: 8 (over z, x), mp: 2 (over core).
Axes of the slice: x: 2, y: 2, z: 4, core: 2. Of those that a mesh axis runs over, the one named last changes fastest.
Arguments:
- tokens: bfloat16 [128, 6144], P(('sweep', 'dp'), 'mp'), parts along dimension 0, may hold values from -6 to 6
- cotangent: bfloat16 [128, 6144], P(('sweep', 'dp'), 'mp'), parts along dimension 0, may hold values from -6 to 6
- inward_blocks: bfloat16 [4, 8, 576, 128, 128], P(('sweep', 'mp'), 'dp'), parts along dimension 0, may hold values from -0.109375 to 0.109375
- inward_rows: int32 [4, 8, 576], P(('sweep', 'mp'), 'dp'), parts along dimension 0, may hold values from 0 to 23, as said below
- inward_cols: int32 [4, 8, 576], P(('sweep', 'mp'), 'dp'), parts along dimension 0, may hold values from 0 to 23
- inward_count: int32 [4, 8], P(('sweep', 'mp'), 'dp'), parts along dimension 0, may hold values from 72 to 576, as said below
- outward_blocks: bfloat16 [16, 2, 576, 128, 128], P(('sweep', 'dp'), 'mp'), parts along dimension 0, may hold values from -0.0546875 to 0.0546875
- outward_rows: int32 [16, 2, 576], P(('sweep', 'dp'), 'mp'), parts along dimension 0, may hold values from 0 to 23, as said below
- outward_cols: int32 [16, 2, 576], P(('sweep', 'dp'), 'mp'), parts along dimension 0, may hold values from 0 to 23
- outward_count: int32 [16, 2], P(('sweep', 'dp'), 'mp'), parts along dimension 0, may hold values from 72 to 576, as said below
Outputs:
- out_tokens: bfloat16 [128, 6144], P(('sweep', 'dp'), 'mp'), parts along dimension 0
- grad_tokens: bfloat16 [128, 6144], P(('sweep', 'dp'), 'mp'), parts along dimension 0
- grad_inward: bfloat16 [4, 8, 576, 128, 128], P(('sweep', 'mp'), 'dp'), parts along dimension 0
- grad_outward: bfloat16 [16, 2, 576, 128, 128], P(('sweep', 'dp'), 'mp'), parts along dimension 0
The draws below stay inside these ranges and needn't reach their ends.
There are 2 independent parts, one for each index of `sweep`. The reference program is written for one: setup_inputs(seed, part) draws one part's arguments, and reference() takes and returns one part's arrays. A program takes and returns all parts, laid end to end along the dimension named above; each array names one. Nothing has to cross between parts.
Inputs may be any that keep to these rules, and one draw needn't show every extreme that they name: In every shard, inward_rows and inward_cols together name each of the 24 x 24 block positions of its region exactly once; the first inward_count slots hold the kept blocks, the others are padding. `inward_count`: some shard keeps all 576 blocks in every draw. In every shard, outward_rows and outward_cols together name each of the 24 x 24 block positions of its region exactly once; the first outward_count slots hold the kept blocks, the others are padding. `outward_count`: some shard keeps all 576 blocks in every draw.
All inputs are finite; a program needn't handle non-finite values.
Results may differ from the reference program's by a relative error of at most 0.0051.
Values may be sent and summed in bfloat16 or wider, within the bound.
No kernel may reach another device: no remote copies, remote signals or barrier semaphores. Data moves between devices by JAX's collectives and lax.ppermute only.
A program may use at most 256 MiB of HBM per device.

```python
import jax
import jax.numpy as jnp

D = 6144
FF = 24576
BS = 128
TOKENS = 64
ROWB = 24
COLB = 24
REGION = 576
N_DP = 8
N_MP = 2


def block_layout(key, shard_total, positions):
    keys = jax.random.split(key, shard_total)
    return jax.vmap(lambda one_key: jax.random.permutation(one_key, positions))(keys).astype(jnp.int32)


def kept_counts(key, shard_total):
    count_key, busy_key = jax.random.split(key)
    counts = jax.random.randint(count_key, (shard_total,), max(1, REGION // 8), REGION, dtype=jnp.int32)
    busiest = jax.random.randint(busy_key, (), 0, shard_total, dtype=jnp.int32)
    return jnp.where(jnp.arange(shard_total, dtype=jnp.int32) == busiest, jnp.int32(REGION), counts)


def draw_inward_rows(key, part):
    order = block_layout(key, N_MP * N_DP, REGION)
    return (order // COLB).reshape(N_MP, N_DP, REGION).astype(jnp.int32)


def draw_inward_cols(key, part):
    order = block_layout(key, N_MP * N_DP, REGION)
    return (order % COLB).reshape(N_MP, N_DP, REGION).astype(jnp.int32)


def draw_inward_count(key, part):
    key = jax.random.fold_in(key, 5)
    return kept_counts(key, N_MP * N_DP).reshape(N_MP, N_DP)


def draw_outward_rows(key, part):
    order = block_layout(jax.random.fold_in(key, 11), N_DP * N_MP, REGION)
    return (order // ROWB).reshape(N_DP, N_MP, REGION).astype(jnp.int32)


def draw_outward_cols(key, part):
    order = block_layout(jax.random.fold_in(key, 11), N_DP * N_MP, REGION)
    return (order % ROWB).reshape(N_DP, N_MP, REGION).astype(jnp.int32)


def draw_outward_count(key, part):
    key = jax.random.fold_in(key, 7)
    return kept_counts(key, N_DP * N_MP).reshape(N_DP, N_MP)


def block_levels(rng, dims, shards, least, largest):
    def one(dim, shards_of):
        steps = jax.random.uniform(jax.random.fold_in(jax.random.fold_in(rng, 6), dim), (shards_of,), jnp.float32, least / len(shards), largest / len(shards))
        return jnp.repeat(jnp.exp(steps), dims[dim] // shards_of).reshape((-1,) + (1,) * (len(dims) - dim - 1))

    level = one(*shards[0])
    for cut in shards[1:]:
        level = level * one(*cut)
    return level


def scatter_about(rng, dims, deviation, most, pieces=(), kind=jnp.bfloat16):
    values = deviation * jax.random.normal(rng, dims, jnp.float32)
    if pieces:
        values = values * block_levels(rng, dims, pieces, -0.22, 0.18)
    return jnp.clip(values, -most, most).astype(kind)


def setup_inputs(seed: int = 0, part: int = 0) -> dict:
    streams_of = jax.random.split(jax.random.key(seed), 11)
    part_splits = jax.random.split(jax.random.fold_in(streams_of[10], part), 11)
    tokens = scatter_about(part_splits[0], (TOKENS, D), 1.0, 6.0, ((0, 8), (1, 2)))
    cotangent = scatter_about(part_splits[1], (TOKENS, D), 1.0, 6.0, ((0, 8), (1, 2)))
    inward_blocks = scatter_about(part_splits[2], (N_MP, N_DP, REGION, BS, BS), (D // 2) ** -0.5, 0.109375, ((0, 2), (1, 8)))
    inward_rows = draw_inward_rows(jax.random.fold_in(jax.random.fold_in(streams_of[10], part), 71), part)
    inward_cols = draw_inward_cols(jax.random.fold_in(jax.random.fold_in(streams_of[10], part), 71), part)
    inward_count = draw_inward_count(jax.random.fold_in(jax.random.fold_in(streams_of[10], part), 71), part)
    outward_blocks = scatter_about(part_splits[6], (N_DP, N_MP, REGION, BS, BS), (FF // 2) ** -0.5, 0.0546875, ((0, 8), (1, 2)))
    outward_rows = draw_outward_rows(jax.random.fold_in(jax.random.fold_in(streams_of[10], part), 71), part)
    outward_cols = draw_outward_cols(jax.random.fold_in(jax.random.fold_in(streams_of[10], part), 71), part)
    outward_count = draw_outward_count(jax.random.fold_in(jax.random.fold_in(streams_of[10], part), 71), part)
    return dict(tokens=tokens, cotangent=cotangent, inward_blocks=inward_blocks, inward_rows=inward_rows, inward_cols=inward_cols, inward_count=inward_count, outward_blocks=outward_blocks, outward_rows=outward_rows, outward_cols=outward_cols, outward_count=outward_count)


root_half = 0.7071067811865476
inv_root_tau = 0.3989422804014327


def gelu_curve(values):
    return 0.5 * values * (1.0 + jax.scipy.special.erf(values * root_half))


def gelu_slope(values):
    return 0.5 * (1.0 + jax.scipy.special.erf(values * root_half)) + values * jnp.exp(-0.5 * values * values) * inv_root_tau


def assemble(blocks, block_rows, block_cols, kept_count, row_blocks, col_blocks):
    outer_size = blocks.shape[0]
    inner_size = blocks.shape[1]
    usable = jnp.arange(REGION)[None, None, :] < kept_count[:, :, None]
    outer = jnp.arange(outer_size)[:, None, None]
    inner = jnp.arange(inner_size)[None, :, None]
    masked = jnp.where(usable[:, :, :, None, None], blocks.astype(jnp.float32), jnp.float32(0.0))
    grid = jnp.zeros((outer_size, inner_size, row_blocks, col_blocks, BS, BS), jnp.float32)
    grid = grid.at[outer, inner, block_rows, block_cols].add(masked)
    whole = grid.transpose(0, 2, 4, 1, 3, 5).reshape(outer_size * row_blocks * BS, inner_size * col_blocks * BS)
    return whole.astype(jnp.bfloat16)


def select(grads, block_rows, block_cols, kept_count, row_blocks, col_blocks):
    outer_size = block_rows.shape[0]
    inner_size = block_rows.shape[1]
    grid_tiles = grads.reshape(outer_size, row_blocks, BS, inner_size, col_blocks, BS).transpose(0, 3, 1, 4, 2, 5)
    outer = jnp.arange(outer_size)[:, None, None]
    inner = jnp.arange(inner_size)[None, :, None]
    picked = grid_tiles[outer, inner, block_rows, block_cols]
    usable = jnp.arange(REGION)[None, None, :] < kept_count[:, :, None]
    return jnp.where(usable[:, :, :, None, None], picked, jnp.float32(0.0)).astype(jnp.bfloat16)


def reference(tokens, cotangent, inward_blocks, inward_rows, inward_cols, inward_count, outward_blocks, outward_rows, outward_cols, outward_count):
    inward = assemble(inward_blocks, inward_rows, inward_cols, inward_count, ROWB, COLB)
    outward = assemble(outward_blocks, outward_rows, outward_cols, outward_count, COLB, ROWB)
    hidden = jnp.dot(tokens, inward, preferred_element_type=jnp.float32)
    activated = gelu_curve(hidden).astype(jnp.bfloat16)
    out_tokens = jnp.dot(activated, outward, preferred_element_type=jnp.float32).astype(jnp.bfloat16)
    grad_act = jnp.dot(cotangent, outward.T, preferred_element_type=jnp.float32)
    grad_hidden = (grad_act * gelu_slope(hidden)).astype(jnp.bfloat16)
    grad_tokens = jnp.dot(grad_hidden, inward.T, preferred_element_type=jnp.float32).astype(jnp.bfloat16)
    grad_scale = float(TOKENS) ** -0.5
    first_grad = jnp.dot(tokens.T, grad_hidden, preferred_element_type=jnp.float32) * grad_scale
    second_grad = jnp.dot(activated.T, cotangent, preferred_element_type=jnp.float32) * grad_scale
    grad_inward = select(first_grad, inward_rows, inward_cols, inward_count, ROWB, COLB)
    grad_outward = select(second_grad, outward_rows, outward_cols, outward_count, COLB, ROWB)
    return (out_tokens, grad_tokens, grad_inward, grad_outward)
```

```python
import functools

import jax
import jax.numpy as jnp
from jax import lax
from jax.experimental import pallas as pl
from jax.experimental.pallas import tpu as pltpu
from jax.sharding import PartitionSpec as P

root_half = 0.7071067811865476
inv_root_tau = 0.3989422804014327

SMEM = pl.BlockSpec(memory_space=pltpu.SMEM)
VMEM = pl.BlockSpec(memory_space=pltpu.VMEM)
ANY = pl.BlockSpec(memory_space=pl.ANY)
MIB = 1 << 20


def gelu_curve(values):
    return 0.5 * values * (1.0 + lax.erf(values * root_half))


def gelu_slope(values):
    return (
        0.5 * (1.0 + lax.erf(values * root_half))
        + values * jnp.exp(-0.5 * values * values) * inv_root_tau
    )


def slots_kernel(row_blocks, col_blocks, in_rows, in_cols, out_rows, out_cols, in_slots, out_slots):
    def place(slot, carry):
        in_slots[in_rows[slot] * col_blocks + in_cols[slot]] = slot
        out_slots[out_rows[slot] * row_blocks + out_cols[slot]] = slot
        return carry

    lax.fori_loop(0, in_rows.shape[0], place, 0, unroll=8)


def slot_maps(in_rows, in_cols, out_rows, out_cols, row_blocks, col_blocks):
    shape = jax.ShapeDtypeStruct(in_rows.shape, jnp.int32)
    return pl.pallas_call(
        functools.partial(slots_kernel, row_blocks, col_blocks),
        out_shape=(shape, shape),
        in_specs=[SMEM] * 4,
        out_specs=(SMEM, SMEM),
        name="slot_maps",
    )(in_rows, in_cols, out_rows, out_cols)


def pair(count):
    return 2 if count % 2 == 0 else 1


def multiply(lhs_ref, blocks_ref, slots_ref, kept, depth, width, across, store):
    side = blocks_ref.shape[-1]
    deep, wide = pair(depth), pair(width)

    def block(k, n):
        position = n * depth + k if across else k * width + n
        slot = slots_ref[position]
        found = blocks_ref[slot]
        return jnp.where(slot < kept, found, jnp.zeros_like(found))

    def column(step, carry):
        n0 = step * wide
        total = None
        for k0 in range(0, depth, deep):
            if across:
                tile = jnp.concatenate(
                    [
                        jnp.concatenate([block(k0 + k, n0 + n) for k in range(deep)], axis=1)
                        for n in range(wide)
                    ],
                    axis=0,
                )
                dims = (((1,), (1,)), ((), ()))
            else:
                tile = jnp.concatenate(
                    [
                        jnp.concatenate([block(k0 + k, n0 + n) for n in range(wide)], axis=1)
                        for k in range(deep)
                    ],
                    axis=0,
                )
                dims = (((1,), (0,)), ((), ()))
            lhs = lhs_ref[:, k0 * side : (k0 + deep) * side]
            part = lax.dot_general(lhs, tile, dims, preferred_element_type=jnp.float32)
            total = part if total is None else total + part
        store(pl.multiple_of(n0 * side, wide * side), wide * side, total)
        return carry

    lax.fori_loop(0, width // wide, column, 0)


def first_kernel(depth, width, across, slots, kept, lhs, blocks, own, sent):
    def store(start, size, total):
        own[:, pl.ds(start, size)] = total
        sent[:, pl.ds(start, size)] = total.astype(jnp.bfloat16)

    multiply(lhs, blocks, slots, kept[0], depth, width, across, store)


def first_product(slots, kept, lhs, blocks, depth, width, across, name):
    shape = (lhs.shape[0], width * blocks.shape[-1])
    return pl.pallas_call(
        functools.partial(first_kernel, depth, width, across),
        out_shape=(jax.ShapeDtypeStruct(shape, jnp.float32), jax.ShapeDtypeStruct(shape, jnp.bfloat16)),
        in_specs=[SMEM, SMEM, VMEM, VMEM],
        out_specs=(VMEM, VMEM),
        compiler_params=pltpu.CompilerParams(vmem_limit_bytes=8 * MIB),
        cost_estimate=pl.CostEstimate(
            flops=2 * lhs.size * width * blocks.shape[-1], bytes_accessed=4 * MIB, transcendentals=0
        ),
        name=name,
    )(slots, kept, lhs, in_vmem(blocks))


def in_vmem(blocks):
    return pltpu.with_memory_space_constraint(blocks, pltpu.VMEM)


def spread(parts, rows):
    def store(start, size, total):
        rounded = total.astype(jnp.bfloat16)
        for index, part in enumerate(parts):
            part[:, pl.ds(start, size)] = rounded[index * rows : (index + 1) * rows]

    return store


def output_kernel(depth, width, rows, slots, kept, own, other, blocks, activated, *parts):
    side = blocks.shape[-1]

    def activate(step, carry):
        at = pl.ds(pl.multiple_of(step * side, side), side)
        hidden = own[:, at] + other[:, at].astype(jnp.float32)
        activated[:, at] = gelu_curve(hidden).astype(jnp.bfloat16)
        return carry

    lax.fori_loop(0, depth, activate, 0)
    multiply(activated, blocks, slots, kept[0], depth, width, False, spread(parts, rows))


def gradient_kernel(
    depth, width, rows, slots, kept, hid_own, hid_other, act_own, act_other, blocks, grad_hidden, *parts
):
    side = blocks.shape[-1]

    def activate(step, carry):
        at = pl.ds(pl.multiple_of(step * side, side), side)
        hidden = hid_own[:, at] + hid_other[:, at].astype(jnp.float32)
        grad_act = act_own[:, at] + act_other[:, at].astype(jnp.float32)
        grad_hidden[:, at] = (grad_act * gelu_slope(hidden)).astype(jnp.bfloat16)
        return carry

    lax.fori_loop(0, depth, activate, 0)
    multiply(grad_hidden, blocks, slots, kept[0], depth, width, True, spread(parts, rows))


def second_product(body, slots, kept, values, blocks, depth, width, pieces, name):
    count = values[0].shape[0]
    side = blocks.shape[-1]
    rows = count // pieces
    shapes = [jax.ShapeDtypeStruct((count, depth * side), jnp.bfloat16)]
    shapes += [jax.ShapeDtypeStruct((rows, width * side), jnp.bfloat16)] * pieces
    middle, *parts = pl.pallas_call(
        functools.partial(body, depth, width, rows),
        out_shape=tuple(shapes),
        in_specs=[SMEM, SMEM] + [VMEM] * (len(values) + 1),
        out_specs=(VMEM,) * len(shapes),
        compiler_params=pltpu.CompilerParams(vmem_limit_bytes=10 * MIB),
        cost_estimate=pl.CostEstimate(
            flops=2 * count * depth * width * side * side, bytes_accessed=6 * MIB, transcendentals=0
        ),
        name=name,
    )(slots, kept, *values, in_vmem(blocks))
    return middle, parts


def outer_kernel(tall, wide, slots, kept_ref, left, right, result, turned, stage, sems):
    count = left.shape[0]
    side = result.shape[-1]
    step_width = pair(wide)
    steps = wide // step_width
    buffers = stage.shape[0]
    kept = kept_ref[0]
    scale = float(count) ** (-0.5)
    zero_at = tall * step_width

    for a in range(tall):
        turned[a] = left[:, a * side : (a + 1) * side].T
    for buffer in range(buffers):
        stage[buffer, zero_at] = jnp.zeros((side, side), jnp.bfloat16)

    def wait(buffer):
        pltpu.make_async_copy(
            stage.at[buffer, pl.ds(0, zero_at)], result.at[pl.ds(0, zero_at)], sems.at[buffer]
        ).wait()

    def step(index, carry):
        buffer = lax.rem(index, buffers)

        @pl.when(index >= buffers)
        def _():
            wait(buffer)

        at = pl.ds(pl.multiple_of(index * step_width * side, step_width * side), step_width * side)
        values = right[:, at]
        for a in range(tall):
            tile = jnp.dot(turned[a], values, preferred_element_type=jnp.float32) * scale
            tile = tile.astype(jnp.bfloat16)
            for b in range(step_width):
                stage[buffer, a * step_width + b] = tile[:, b * side : (b + 1) * side]
                slot = slots[a * wide + index * step_width + b]
                source = jnp.where(slot < kept, a * step_width + b, zero_at)
                pltpu.make_async_copy(
                    stage.at[buffer, source], result.at[slot], sems.at[buffer]
                ).start()
        return carry

    lax.fori_loop(0, steps, step, 0)
    for index in range(max(0, steps - buffers), steps):
        wait(index % buffers)


def outer_product(slots, kept, left, right, side, name):
    count = left.shape[0]
    tall, wide = left.shape[1] // side, right.shape[1] // side
    buffers = min(3, wide // pair(wide))
    return pl.pallas_call(
        functools.partial(outer_kernel, tall, wide),
        out_shape=jax.ShapeDtypeStruct((tall * wide, side, side), jnp.bfloat16),
        in_specs=[SMEM, SMEM, VMEM, VMEM],
        out_specs=ANY,
        scratch_shapes=[
            pltpu.VMEM((tall, side, count), jnp.bfloat16),
            pltpu.VMEM((buffers, tall * pair(wide) + 1, side, side), jnp.bfloat16),
            pltpu.SemaphoreType.DMA((buffers,)),
        ],
        compiler_params=pltpu.CompilerParams(vmem_limit_bytes=14 * MIB),
        cost_estimate=pl.CostEstimate(
            flops=8 * left.size * right.shape[1],
            bytes_accessed=2 * tall * wide * side * side,
            transcendentals=0,
        ),
        name=name,
    )(slots, kept, left, right)


def gather(values, devices):
    if devices > 8:
        return lax.all_gather(values, "dp", axis=0, tiled=True)
    pieces = [values]
    for away in range(1, devices):
        path = [(i, (i + away) % devices) for i in range(devices)]
        pieces.append(lax.ppermute(values, "dp", path))
    return jnp.concatenate(pieces, axis=0)


def scatter(parts, devices):
    if devices > 8:
        whole = jnp.concatenate(parts, axis=0).astype(jnp.float32)
        return lax.psum_scatter(whole, "dp", scatter_dimension=0, tiled=True).astype(jnp.bfloat16)
    total = parts[0].astype(jnp.float32)
    for away in range(1, devices):
        path = [(i, (i - away) % devices) for i in range(devices)]
        total = total + lax.ppermute(parts[away], "dp", path).astype(jnp.float32)
    return total.astype(jnp.bfloat16)


def swap(values, devices):
    return lax.ppermute(values, "mp", [(i, (i + 1) % devices) for i in range(devices)])


def shards(
    tokens,
    cotangent,
    inward_blocks,
    inward_rows,
    inward_cols,
    inward_count,
    outward_blocks,
    outward_rows,
    outward_cols,
    outward_count,
):
    side = inward_blocks.shape[-1]
    region = inward_blocks.shape[2]
    row_blocks = tokens.shape[1] // side
    col_blocks = region // row_blocks
    n_dp = lax.axis_size("dp")
    n_mp = lax.axis_size("mp")
    in_kept = inward_count.reshape(1)
    out_kept = outward_count.reshape(1)
    inward = inward_blocks.reshape(region, side, side)
    outward = outward_blocks.reshape(region, side, side)
    in_slots, out_slots = slot_maps(
        inward_rows.reshape(region),
        inward_cols.reshape(region),
        outward_rows.reshape(region),
        outward_cols.reshape(region),
        row_blocks,
        col_blocks,
    )
    all_tokens = gather(tokens, n_dp)
    all_grads = gather(cotangent, n_dp)
    hid_own, hid_sent = first_product(
        in_slots, in_kept, all_tokens, inward, row_blocks, col_blocks, False, "hidden"
    )
    hid_other = swap(hid_sent, n_mp)
    act_own, act_sent = first_product(
        out_slots, out_kept, all_grads, outward, row_blocks, col_blocks, True, "grad_act"
    )
    act_other = swap(act_sent, n_mp)
    activated, out_parts = second_product(
        output_kernel, out_slots, out_kept, (hid_own, hid_other), outward, col_blocks, row_blocks, n_dp, "output"
    )
    out_tokens = scatter(out_parts, n_dp)
    grad_hidden, in_parts = second_product(
        gradient_kernel,
        in_slots,
        in_kept,
        (hid_own, hid_other, act_own, act_other),
        inward,
        col_blocks,
        row_blocks,
        n_dp,
        "grad_tokens",
    )
    grad_tokens = scatter(in_parts, n_dp)
    grad_outward = outer_product(out_slots, out_kept, activated, all_grads, side, "outward")
    grad_inward = outer_product(in_slots, in_kept, all_tokens, grad_hidden, side, "inward")
    return (
        out_tokens,
        grad_tokens,
        grad_inward.reshape(inward_blocks.shape),
        grad_outward.reshape(outward_blocks.shape),
    )


def solution(mesh):
    in_specs = (
        P(("sweep", "dp"), "mp"),
        P(("sweep", "dp"), "mp"),
        P(("sweep", "mp"), "dp", None, None, None),
        P(("sweep", "mp"), "dp", None),
        P(("sweep", "mp"), "dp", None),
        P(("sweep", "mp"), "dp"),
        P(("sweep", "dp"), "mp", None, None, None),
        P(("sweep", "dp"), "mp", None),
        P(("sweep", "dp"), "mp", None),
        P(("sweep", "dp"), "mp"),
    )
    out_specs = (
        P(("sweep", "dp"), "mp"),
        P(("sweep", "dp"), "mp"),
        P(("sweep", "mp"), "dp", None, None, None),
        P(("sweep", "dp"), "mp", None, None, None),
    )
    return jax.shard_map(shards, mesh=mesh, in_specs=in_specs, out_specs=out_specs, check_vma=False)
```

```python
import functools

import jax
import jax.numpy as jnp
from jax import lax
from jax.experimental import pallas as pl
from jax.experimental.pallas import tpu as pltpu
from jax.sharding import PartitionSpec as P

root_half = 0.7071067811865476
inv_root_tau = 0.3989422804014327

SMEM = pl.BlockSpec(memory_space=pltpu.SMEM)
VMEM = pl.BlockSpec(memory_space=pltpu.VMEM)
ANY = pl.BlockSpec(memory_space=pl.ANY)
HBM = pl.BlockSpec(memory_space=pltpu.HBM)
GRANT = 4 << 20


def gelu_curve(values):
    return 0.5 * values * (1.0 + lax.erf(values * root_half))


def gelu_slope(values):
    return (
        0.5 * (1.0 + lax.erf(values * root_half))
        + values * jnp.exp(-0.5 * values * values) * inv_root_tau
    )


def slots_kernel(width, rows, cols, earlier, slots, rows_near, cols_near, sems):
    copies = [
        pltpu.make_async_copy(rows, rows_near, sems.at[0]),
        pltpu.make_async_copy(cols, cols_near, sems.at[1]),
    ]
    for copy in copies:
        copy.start()
    for copy in copies:
        copy.wait()

    def place(slot, carry):
        slots[rows_near[0, 0, slot] * width + cols_near[0, 0, slot]] = slot
        return carry

    lax.fori_loop(0, rows.shape[2], place, 0, unroll=16 if rows.shape[2] % 16 == 0 else 8)


def slot_map(rows, cols, width, earlier, name):
    return pl.pallas_call(
        functools.partial(slots_kernel, width),
        out_shape=jax.ShapeDtypeStruct(rows.shape[2:], jnp.int32),
        in_specs=[HBM, HBM, ANY],
        out_specs=SMEM,
        scratch_shapes=[
            pltpu.SMEM(rows.shape, rows.dtype),
            pltpu.SMEM(cols.shape, cols.dtype),
            pltpu.SemaphoreType.DMA((2,)),
        ],
        compiler_params=pltpu.CompilerParams(vmem_limit_bytes=GRANT),
        cost_estimate=pl.CostEstimate(flops=0, bytes_accessed=6 << 20, transcendentals=0),
        name=name,
    )(in_hbm(rows), in_hbm(cols), earlier)


def pair(count):
    return 2 if count % 2 == 0 else 1


def product(lhs_ref, block, side, depth, deep, wide, across):
    total = None
    for k0 in range(0, depth, deep):
        if across:
            tile = jnp.concatenate(
                [jnp.concatenate([block(k0 + k, n) for k in range(deep)], axis=1) for n in range(wide)],
                axis=0,
            )
            dims = (((1,), (1,)), ((), ()))
        else:
            tile = jnp.concatenate(
                [jnp.concatenate([block(k0 + k, n) for n in range(wide)], axis=1) for k in range(deep)],
                axis=0,
            )
            dims = (((1,), (0,)), ((), ()))
        lhs = lhs_ref[:, k0 * side : (k0 + deep) * side]
        part = lax.dot_general(lhs, tile, dims, preferred_element_type=jnp.float32)
        total = part if total is None else total + part
    return total


def multiply(lhs_ref, blocks_ref, slots_ref, kept, depth, width, across, store):
    side = blocks_ref.shape[-1]
    deep, wide = pair(depth), pair(width)

    def column(step, carry):
        n0 = step * wide

        def block(k, n):
            slot = slots_ref[(n0 + n) * depth + k if across else k * width + n0 + n]
            found = blocks_ref[slot]
            return jnp.where(slot < kept, found, jnp.zeros_like(found))

        total = product(lhs_ref, block, side, depth, deep, wide, across)
        store(pl.multiple_of(n0 * side, wide * side), wide * side, total)
        return carry

    steps = width // wide
    lax.fori_loop(0, steps, column, 0, unroll=pair(steps))


def stream(lhs_ref, blocks_ref, slots_ref, kept, depth, width, across, store, fetched, sems):
    side = blocks_ref.shape[-1]
    deep = pair(depth)
    buffers = fetched.shape[0]
    wide = fetched.shape[1] // depth
    steps = width // wide

    def slot(step, k, n):
        column = step * wide + n
        return slots_ref[column * depth + k if across else k * width + column]

    def fetch(step, buffer):
        for n in range(wide):
            for k in range(depth):
                pltpu.make_async_copy(
                    blocks_ref.at[slot(step, k, n)], fetched.at[buffer, k * wide + n], sems.at[buffer]
                ).start()

    def column(step, buffer):
        pltpu.make_async_copy(
            blocks_ref.at[pl.ds(0, depth * wide)], fetched.at[buffer], sems.at[buffer]
        ).wait()

        def block(k, n):
            found = fetched[buffer, k * wide + n]
            return jnp.where(slot(step, k, n) < kept, found, jnp.zeros_like(found))

        store(
            pl.multiple_of(step * wide * side, wide * side),
            wide * side,
            product(lhs_ref, block, side, depth, deep, wide, across),
        )

    ahead = buffers - 1
    for step in range(ahead):
        fetch(step, step)

    def both(step, carry):
        fetch(step + ahead, lax.rem(step + ahead, buffers))
        column(step, lax.rem(step, buffers))
        return carry

    lax.fori_loop(0, steps - ahead, both, 0)
    for step in range(steps - ahead, steps):
        column(step, step % buffers)


def first_kernel(depth, width, across, slots, kept, lhs, blocks, earlier, own, sent, *fetch):
    def store(start, size, total):
        own[:, pl.ds(start, size)] = total
        sent[:, pl.ds(start, size)] = total.astype(jnp.bfloat16)

    run = stream if fetch else multiply
    run(lhs, blocks, slots, kept[0, 0], depth, width, across, store, *fetch)


def first_product(slots, kept, lhs, blocks, earlier, depth, width, across, streamed, name):
    side = blocks.shape[-1]
    shape = (lhs.shape[0], width * side)
    scratch, grant = [], GRANT
    if streamed:
        wide = next(size for size in (4, 3, 2, 1) if width % size == 0)
        buffers = min(3, width // wide)
        scratch = [
            pltpu.VMEM((buffers, depth * wide, side, side), blocks.dtype),
            pltpu.SemaphoreType.DMA((buffers,)),
        ]
        grant = 16 << 20
    return pl.pallas_call(
        functools.partial(first_kernel, depth, width, across),
        out_shape=(jax.ShapeDtypeStruct(shape, jnp.float32), jax.ShapeDtypeStruct(shape, jnp.bfloat16)),
        in_specs=[SMEM, SMEM, VMEM, HBM if streamed else VMEM, ANY],
        out_specs=(VMEM, VMEM),
        scratch_shapes=scratch,
        compiler_params=pltpu.CompilerParams(vmem_limit_bytes=grant),
        cost_estimate=pl.CostEstimate(
            flops=2 * lhs.size * width * side, bytes_accessed=2 * blocks.size, transcendentals=0
        ),
        name=name,
    )(slots, kept, lhs, in_hbm(blocks) if streamed else in_vmem(blocks), earlier)


def in_hbm(values):
    return pltpu.with_memory_space_constraint(values, pltpu.HBM)


def in_vmem(blocks):
    return pltpu.with_memory_space_constraint(blocks, pltpu.VMEM)


def spread(parts, rows, start_row):
    def store(start, size, total):
        rounded = total.astype(jnp.bfloat16)
        for index, part in enumerate(parts):
            part[start_row : start_row + rows, pl.ds(start, size)] = rounded[index * rows : (index + 1) * rows]

    return store


def output_kernel(depth, width, rows, slots, kept, own, other, blocks, earlier, activated, *parts):
    side = blocks.shape[-1]

    def activate(step, carry):
        at = pl.ds(pl.multiple_of(step * side, side), side)
        hidden = own[:, at] + other[:, at].astype(jnp.float32)
        activated[:, at] = gelu_curve(hidden).astype(jnp.bfloat16)
        return carry

    lax.fori_loop(0, depth, activate, 0)
    multiply(activated, blocks, slots, kept[0, 0], depth, width, False, spread(parts, rows, 0))


def output_product(slots, kept, own, other, blocks, earlier, depth, width, pieces):
    count = own.shape[0]
    side = blocks.shape[-1]
    rows = count // pieces
    shapes = [jax.ShapeDtypeStruct((count, depth * side), jnp.bfloat16)]
    shapes += [jax.ShapeDtypeStruct((rows, width * side), jnp.bfloat16)] * pieces
    activated, *parts = pl.pallas_call(
        functools.partial(output_kernel, depth, width, rows),
        out_shape=tuple(shapes),
        in_specs=[SMEM, SMEM, VMEM, VMEM, VMEM, ANY],
        out_specs=(VMEM,) * len(shapes),
        compiler_params=pltpu.CompilerParams(vmem_limit_bytes=GRANT),
        cost_estimate=pl.CostEstimate(
            flops=2 * count * depth * width * side * side, bytes_accessed=2 * blocks.size, transcendentals=0
        ),
        name="output",
    )(slots, kept, own, other, in_vmem(blocks), earlier)
    return activated, parts


def gradient_kernel(depth, width, rows, pieces, slots, kept, hid_own, hid_other, act_own, act_other, blocks, *refs):
    out_parts, (grad_hidden, *both) = refs[:pieces], refs[pieces:]
    side = blocks.shape[-1]

    def activate(step, carry):
        at = pl.ds(pl.multiple_of(step * side, side), side)
        hidden = hid_own[:, at] + hid_other[:, at].astype(jnp.float32)
        grad_act = act_own[:, at] + act_other[:, at].astype(jnp.float32)
        grad_hidden[:, at] = (grad_act * gelu_slope(hidden)).astype(jnp.bfloat16)
        return carry

    lax.fori_loop(0, depth, activate, 0)
    for part, out_part in zip(both, out_parts):
        part[:rows] = out_part[...]
    multiply(grad_hidden, blocks, slots, kept[0, 0], depth, width, True, spread(both, rows, rows))


def gradient_product(slots, kept, values, blocks, out_parts, depth, width):
    count = values[0].shape[0]
    side = blocks.shape[-1]
    pieces = len(out_parts)
    rows = count // pieces
    shapes = [jax.ShapeDtypeStruct((count, depth * side), jnp.bfloat16)]
    shapes += [jax.ShapeDtypeStruct((2 * rows, width * side), jnp.bfloat16)] * pieces
    grad_hidden, *both = pl.pallas_call(
        functools.partial(gradient_kernel, depth, width, rows, pieces),
        out_shape=tuple(shapes),
        in_specs=[SMEM, SMEM] + [VMEM] * (5 + pieces),
        out_specs=(VMEM,) * len(shapes),
        compiler_params=pltpu.CompilerParams(vmem_limit_bytes=GRANT),
        cost_estimate=pl.CostEstimate(
            flops=2 * count * depth * width * side * side, bytes_accessed=2 * blocks.size, transcendentals=0
        ),
        name="grad_tokens",
    )(slots, kept, *values, in_vmem(blocks), *out_parts)
    return grad_hidden, both


def outer_kernel(tall, wide, slots, kept_ref, left, right, earlier, result, turned, stage, sems):
    count = left.shape[0]
    side = result.shape[-1]
    step_width = stage.shape[1] // tall
    steps = wide // step_width
    buffers = stage.shape[0]
    kept = kept_ref[0, 0]
    scale = float(count) ** (-0.5)
    zero_at = tall * step_width

    for a in range(tall):
        turned[a] = left[:, a * side : (a + 1) * side].T
    for buffer in range(buffers):
        stage[buffer, zero_at] = jnp.zeros((side, side), jnp.bfloat16)

    def wait(buffer):
        pltpu.make_async_copy(
            stage.at[buffer, pl.ds(0, zero_at)], result.at[pl.ds(0, zero_at)], sems.at[buffer]
        ).wait()

    def step(index, carry):
        buffer = lax.rem(index, buffers)

        @pl.when(index >= buffers)
        def _():
            wait(buffer)

        at = pl.ds(pl.multiple_of(index * step_width * side, step_width * side), step_width * side)
        values = right[:, at]
        for a in range(tall):
            tile = jnp.dot(turned[a], values, preferred_element_type=jnp.float32) * scale
            tile = tile.astype(jnp.bfloat16)
            for b in range(step_width):
                stage[buffer, a * step_width + b] = tile[:, b * side : (b + 1) * side]
                slot = slots[a * wide + index * step_width + b]
                source = jnp.where(slot < kept, a * step_width + b, zero_at)
                pltpu.make_async_copy(
                    stage.at[buffer, source], result.at[slot], sems.at[buffer]
                ).start()
        return carry

    lax.fori_loop(0, steps, step, 0)
    for index in range(max(0, steps - buffers), steps):
        wait(index % buffers)


def outer_product(slots, kept, left, right, side, earlier, name):
    count = left.shape[0]
    tall, wide = left.shape[1] // side, right.shape[1] // side
    step_width = next(size for size in (6, 4, 3, 2, 1) if wide % size == 0)
    buffers = min(2, wide // step_width)
    return pl.pallas_call(
        functools.partial(outer_kernel, tall, wide),
        out_shape=jax.ShapeDtypeStruct((tall * wide, side, side), jnp.bfloat16),
        in_specs=[SMEM, SMEM, VMEM, VMEM, ANY],
        out_specs=ANY,
        scratch_shapes=[
            pltpu.VMEM((tall, side, count), jnp.bfloat16),
            pltpu.VMEM((buffers, tall * step_width + 1, side, side), jnp.bfloat16),
            pltpu.SemaphoreType.DMA((buffers,)),
        ],
        compiler_params=pltpu.CompilerParams(vmem_limit_bytes=16 << 20),
        cost_estimate=pl.CostEstimate(
            flops=8 * left.size * right.shape[1],
            bytes_accessed=2 * tall * wide * side * side,
            transcendentals=0,
        ),
        name=name,
    )(slots, kept, left, right, earlier)


def exchange(values, away, devices):
    return lax.ppermute(values, "dp", [(i, i ^ away) for i in range(devices)])


def gather(values, devices):
    if devices != 8:
        return lax.all_gather(values, "dp", axis=0, tiled=True), values
    near = jnp.concatenate([values, exchange(values, 4, devices)], axis=0)
    rest = [exchange(near, away, devices) for away in (2, 3, 1)]
    return jnp.concatenate([near] + rest, axis=0), near


def near_sum(parts, devices):
    total = parts[0].astype(jnp.float32)
    for part, away in zip(parts[1:], (2, 3, 1)):
        total = total + exchange(part, away, devices).astype(jnp.float32)
    return total


def far_sum(total, rows, devices):
    mine = [total[0:rows], total[2 * rows : 3 * rows]]
    theirs = jnp.concatenate([total[rows : 2 * rows], total[3 * rows :]], axis=0).astype(jnp.bfloat16)
    far = exchange(theirs, 4, devices).astype(jnp.float32)
    return [(mine[i] + far[i * rows : (i + 1) * rows]).astype(jnp.bfloat16) for i in range(2)]


def full_sum(both, rows):
    results = []
    for first in (0, rows):
        whole = jnp.concatenate([part[first : first + rows] for part in both], axis=0)
        summed = lax.psum_scatter(whole.astype(jnp.float32), "dp", scatter_dimension=0, tiled=True)
        results.append(summed.astype(jnp.bfloat16))
    return results


def swap(values, devices):
    return lax.ppermute(values, "mp", [(i, (i + 1) % devices) for i in range(devices)])


def shards(
    tokens,
    cotangent,
    inward_blocks,
    inward_rows,
    inward_cols,
    inward_count,
    outward_blocks,
    outward_rows,
    outward_cols,
    outward_count,
):
    side = inward_blocks.shape[-1]
    region = inward_blocks.shape[2]
    row_blocks = tokens.shape[1] // side
    col_blocks = region // row_blocks
    n_dp = lax.axis_size("dp")
    n_mp = lax.axis_size("mp")
    pieces = 4 if n_dp == 8 else n_dp
    in_kept, out_kept = inward_count, outward_count
    inward = inward_blocks.reshape(region, side, side)
    outward = outward_blocks.reshape(region, side, side)
    in_slots = slot_map(inward_rows, inward_cols, col_blocks, in_kept, "in_slots")
    all_tokens, near = gather(tokens, n_dp)
    all_grads, _ = gather(cotangent, n_dp)
    out_slots = slot_map(outward_rows, outward_cols, row_blocks, near, "out_slots")
    hid_own, hid_sent = first_product(
        in_slots, in_kept, all_tokens, inward, in_kept, row_blocks, col_blocks, False, True, "hidden"
    )
    hid_other = swap(hid_sent, n_mp)
    act_own, act_sent = first_product(
        out_slots, out_kept, all_grads, outward, hid_own, row_blocks, col_blocks, True, False, "grad_act"
    )
    act_other = swap(act_sent, n_mp)
    activated, out_parts = output_product(
        out_slots, out_kept, hid_own, hid_other, outward, act_own, col_blocks, row_blocks, pieces
    )
    grad_hidden, both = gradient_product(
        in_slots, in_kept, (hid_own, hid_other, act_own, act_other), inward, out_parts, col_blocks, row_blocks
    )
    rows = tokens.shape[0]
    nearly = near_sum(both, n_dp) if n_dp == 8 else in_kept
    grad_outward = outer_product(out_slots, out_kept, activated, all_grads, side, grad_hidden, "outward")
    grad_inward = outer_product(in_slots, in_kept, all_tokens, grad_hidden, side, nearly, "inward")
    out_tokens, grad_tokens = far_sum(nearly, rows, n_dp) if n_dp == 8 else full_sum(both, rows)
    return (
        out_tokens,
        grad_tokens,
        grad_inward.reshape(inward_blocks.shape),
        grad_outward.reshape(outward_blocks.shape),
    )


def solution(mesh):
    in_specs = (
        P(("sweep", "dp"), "mp"),
        P(("sweep", "dp"), "mp"),
        P(("sweep", "mp"), "dp", None, None, None),
        P(("sweep", "mp"), "dp", None),
        P(("sweep", "mp"), "dp", None),
        P(("sweep", "mp"), "dp"),
        P(("sweep", "dp"), "mp", None, None, None),
        P(("sweep", "dp"), "mp", None),
        P(("sweep", "dp"), "mp", None),
        P(("sweep", "dp"), "mp"),
    )
    out_specs = (
        P(("sweep", "dp"), "mp"),
        P(("sweep", "dp"), "mp"),
        P(("sweep", "mp"), "dp", None, None, None),
        P(("sweep", "dp"), "mp", None, None, None),
    )
    return jax.shard_map(shards, mesh=mesh, in_specs=in_specs, out_specs=out_specs, check_vma=False)
```

```python
import functools

import jax
import jax.numpy as jnp
from jax import lax
from jax.experimental import pallas as pl
from jax.experimental.pallas import tpu as pltpu
from jax.sharding import PartitionSpec as P

root_half = 0.7071067811865476
inv_root_tau = 0.3989422804014327

SMEM = pl.BlockSpec(memory_space=pltpu.SMEM)
VMEM = pl.BlockSpec(memory_space=pltpu.VMEM)
ANY = pl.BlockSpec(memory_space=pl.ANY)
HBM = pl.BlockSpec(memory_space=pltpu.HBM)
GRANT = 4 << 20


def gelu_curve(values):
    return 0.5 * values * (1.0 + lax.erf(values * root_half))


def gelu_slope(values):
    return (
        0.5 * (1.0 + lax.erf(values * root_half))
        + values * jnp.exp(-0.5 * values * values) * inv_root_tau
    )


def slots_kernel(widths, *refs):
    far, counts, slots, near, (spread_out, sems) = refs[:4], refs[4:6], refs[6:8], refs[8:12], refs[12:]
    copies = [pltpu.make_async_copy(*ends, sems.at[index]) for index, ends in enumerate(zip(far, near))]
    for copy in copies:
        copy.start()
    for copy in copies:
        copy.wait()
    region = near[0].shape[-1]
    lanes = spread_out.shape[-1]
    side = 128
    down = lax.broadcasted_iota(jnp.int32, (side, side), 0)
    along = lax.broadcasted_iota(jnp.int32, (side, side), 1)
    positions = lax.broadcasted_iota(jnp.int32, (side, lanes), 1)
    for which, width in enumerate(widths):
        rows, cols, kept = near[2 * which], near[2 * which + 1], counts[which]
        spread_out[...] = jnp.full(spread_out.shape, -1, jnp.int32)
        spread_out[0:1, 0:region] = rows[0] * width + cols[0]
        total = jnp.zeros((1, lanes), jnp.int32)
        for start in range(0, lanes, side):
            there = jnp.broadcast_to(spread_out[0:1, start : start + side], (side, side))
            column = jnp.sum(jnp.where(down == along, there, 0), axis=1, keepdims=True)
            slot = lax.broadcasted_iota(jnp.int32, (side, lanes), 0) + start
            code = jnp.where(slot < kept[0, 0], slot, slot - region)
            total += jnp.sum(jnp.where(column == positions, code, 0), axis=0, keepdims=True)
        slots[which][...] = total[:, 0:region]


def slot_maps(places, counts, in_width, out_width):
    region = places[0].shape[-1]
    lanes = -(-region // 128) * 128
    shape = jax.ShapeDtypeStruct((1, region), jnp.int32)
    near = [pltpu.VMEM(place.shape, place.dtype) for place in places]
    return pl.pallas_call(
        functools.partial(slots_kernel, (in_width, out_width)),
        out_shape=(shape, shape),
        in_specs=[HBM] * 4 + [SMEM] * 2,
        out_specs=(VMEM, VMEM),
        scratch_shapes=near + [pltpu.VMEM((8, lanes), jnp.int32), pltpu.SemaphoreType.DMA((4,))],
        compiler_params=pltpu.CompilerParams(vmem_limit_bytes=GRANT),
        cost_estimate=pl.CostEstimate(flops=0, bytes_accessed=4 << 20, transcendentals=0),
        name="slot_maps",
    )(*[in_hbm(place) for place in places], *counts)


def pair(count):
    return 2 if count % 2 == 0 else 1


def product(lhs_ref, block, side, depth, deep, wide, across):
    total = None
    for k0 in range(0, depth, deep):
        if across:
            tile = jnp.concatenate(
                [jnp.concatenate([block(k0 + k, n) for k in range(deep)], axis=1) for n in range(wide)],
                axis=0,
            )
            dims = (((1,), (1,)), ((), ()))
        else:
            tile = jnp.concatenate(
                [jnp.concatenate([block(k0 + k, n) for n in range(wide)], axis=1) for k in range(deep)],
                axis=0,
            )
            dims = (((1,), (0,)), ((), ()))
        lhs = lhs_ref[:, k0 * side : (k0 + deep) * side]
        part = lax.dot_general(lhs, tile, dims, preferred_element_type=jnp.float32)
        total = part if total is None else total + part
    return total


def multiply(lhs_ref, blocks_ref, slots_ref, depth, width, across, store):
    side = blocks_ref.shape[-1]
    deep, wide = pair(depth), pair(width)

    def column(step, carry):
        n0 = step * wide

        def block(k, n):
            slot = slots_ref[0, (n0 + n) * depth + k if across else k * width + n0 + n]
            found = blocks_ref[jnp.maximum(slot, 0)]
            return jnp.where(slot >= 0, found, jnp.zeros_like(found))

        total = product(lhs_ref, block, side, depth, deep, wide, across)
        store(pl.multiple_of(n0 * side, wide * side), wide * side, total)
        return carry

    steps = width // wide
    lax.fori_loop(0, steps, column, 0, unroll=pair(steps))


def stream(lhs_ref, blocks_ref, slots_ref, depth, width, across, store, fetched, sems):
    side = blocks_ref.shape[-1]
    deep = pair(depth)
    buffers = fetched.shape[0]
    wide = fetched.shape[1] // depth
    steps = width // wide

    def slot(step, k, n):
        column = step * wide + n
        return slots_ref[0, column * depth + k if across else k * width + column]

    def fetch(step, buffer):
        for n in range(wide):
            for k in range(depth):
                code = slot(step, k, n)
                source = jnp.where(code >= 0, code, code + blocks_ref.shape[0])
                pltpu.make_async_copy(
                    blocks_ref.at[source], fetched.at[buffer, k * wide + n], sems.at[buffer]
                ).start()

    def column(step, buffer):
        pltpu.make_async_copy(
            blocks_ref.at[pl.ds(0, depth * wide)], fetched.at[buffer], sems.at[buffer]
        ).wait()

        def block(k, n):
            found = fetched[buffer, k * wide + n]
            return jnp.where(slot(step, k, n) >= 0, found, jnp.zeros_like(found))

        store(
            pl.multiple_of(step * wide * side, wide * side),
            wide * side,
            product(lhs_ref, block, side, depth, deep, wide, across),
        )

    ahead = buffers - 1
    for step in range(ahead):
        fetch(step, step)

    def both(step, carry):
        fetch(step + ahead, lax.rem(step + ahead, buffers))
        column(step, lax.rem(step, buffers))
        return carry

    lax.fori_loop(0, steps - ahead, both, 0)
    for step in range(steps - ahead, steps):
        column(step, step % buffers)


def first_kernel(depth, width, across, slots, lhs, blocks, earlier, own, sent, *fetch):
    def store(start, size, total):
        own[:, pl.ds(start, size)] = total
        sent[:, pl.ds(start, size)] = total.astype(jnp.bfloat16)

    run = stream if fetch else multiply
    run(lhs, blocks, slots, depth, width, across, store, *fetch)


def first_product(slots, lhs, blocks, earlier, depth, width, across, streamed, name):
    side = blocks.shape[-1]
    shape = (lhs.shape[0], width * side)
    scratch, grant = [], GRANT
    if streamed:
        wide = next(size for size in (4, 3, 2, 1) if width % size == 0)
        buffers = min(3, width // wide)
        scratch = [
            pltpu.VMEM((buffers, depth * wide, side, side), blocks.dtype),
            pltpu.SemaphoreType.DMA((buffers,)),
        ]
        grant = 16 << 20
    return pl.pallas_call(
        functools.partial(first_kernel, depth, width, across),
        out_shape=(jax.ShapeDtypeStruct(shape, jnp.float32), jax.ShapeDtypeStruct(shape, jnp.bfloat16)),
        in_specs=[SMEM, VMEM, HBM if streamed else VMEM, ANY],
        out_specs=(VMEM, VMEM),
        scratch_shapes=scratch,
        compiler_params=pltpu.CompilerParams(vmem_limit_bytes=grant),
        cost_estimate=pl.CostEstimate(
            flops=2 * lhs.size * width * side, bytes_accessed=2 * blocks.size, transcendentals=0
        ),
        name=name,
    )(slots, lhs, in_hbm(blocks) if streamed else in_vmem(blocks), earlier)


def in_hbm(values):
    return pltpu.with_memory_space_constraint(values, pltpu.HBM)


def in_vmem(blocks):
    return pltpu.with_memory_space_constraint(blocks, pltpu.VMEM)


def spread(parts, rows, start_row):
    def store(start, size, total):
        rounded = total.astype(jnp.bfloat16)
        for index, part in enumerate(parts):
            part[start_row : start_row + rows, pl.ds(start, size)] = rounded[index * rows : (index + 1) * rows]

    return store


def output_kernel(depth, width, rows, slots, own, other, blocks, earlier, activated, *parts):
    side = blocks.shape[-1]

    def activate(step, carry):
        at = pl.ds(pl.multiple_of(step * side, side), side)
        hidden = own[:, at] + other[:, at].astype(jnp.float32)
        activated[:, at] = gelu_curve(hidden).astype(jnp.bfloat16)
        return carry

    lax.fori_loop(0, depth, activate, 0)
    multiply(activated, blocks, slots, depth, width, False, spread(parts, rows, 0))


def output_product(slots, own, other, blocks, earlier, depth, width, pieces):
    count = own.shape[0]
    side = blocks.shape[-1]
    rows = count // pieces
    shapes = [jax.ShapeDtypeStruct((count, depth * side), jnp.bfloat16)]
    shapes += [jax.ShapeDtypeStruct((rows, width * side), jnp.bfloat16)] * pieces
    activated, *parts = pl.pallas_call(
        functools.partial(output_kernel, depth, width, rows),
        out_shape=tuple(shapes),
        in_specs=[SMEM, VMEM, VMEM, VMEM, ANY],
        out_specs=(VMEM,) * len(shapes),
        compiler_params=pltpu.CompilerParams(vmem_limit_bytes=GRANT),
        cost_estimate=pl.CostEstimate(
            flops=2 * count * depth * width * side * side, bytes_accessed=2 * blocks.size, transcendentals=0
        ),
        name="output",
    )(slots, own, other, in_vmem(blocks), earlier)
    return activated, parts


def gradient_kernel(depth, width, rows, pieces, slots, hid_own, hid_other, act_own, act_other, blocks, *refs):
    out_parts, (grad_hidden, *both) = refs[:pieces], refs[pieces:]
    side = blocks.shape[-1]

    def activate(step, carry):
        at = pl.ds(pl.multiple_of(step * side, side), side)
        hidden = hid_own[:, at] + hid_other[:, at].astype(jnp.float32)
        grad_act = act_own[:, at] + act_other[:, at].astype(jnp.float32)
        grad_hidden[:, at] = (grad_act * gelu_slope(hidden)).astype(jnp.bfloat16)
        return carry

    lax.fori_loop(0, depth, activate, 0)
    for part, out_part in zip(both, out_parts):
        part[:rows] = out_part[...]
    multiply(grad_hidden, blocks, slots, depth, width, True, spread(both, rows, rows))


def gradient_product(slots, values, blocks, out_parts, depth, width):
    count = values[0].shape[0]
    side = blocks.shape[-1]
    pieces = len(out_parts)
    rows = count // pieces
    shapes = [jax.ShapeDtypeStruct((count, depth * side), jnp.bfloat16)]
    shapes += [jax.ShapeDtypeStruct((2 * rows, width * side), jnp.bfloat16)] * pieces
    grad_hidden, *both = pl.pallas_call(
        functools.partial(gradient_kernel, depth, width, rows, pieces),
        out_shape=tuple(shapes),
        in_specs=[SMEM] + [VMEM] * (5 + pieces),
        out_specs=(VMEM,) * len(shapes),
        compiler_params=pltpu.CompilerParams(vmem_limit_bytes=GRANT),
        cost_estimate=pl.CostEstimate(
            flops=2 * count * depth * width * side * side, bytes_accessed=2 * blocks.size, transcendentals=0
        ),
        name="grad_tokens",
    )(slots, *values, in_vmem(blocks), *out_parts)
    return grad_hidden, both


def outer_steps(job, begin, end, used, slots, left, right, result, turned, stage, sems):
    tall, wide, step_width = job
    count = left.shape[0]
    side = result.shape[-1]
    region = tall * wide
    buffers = stage.shape[0]
    scale = float(count) ** (-0.5)
    zero_at = stage.shape[1] - 1
    for a in range(tall):
        turned[a] = left[:, a * side : (a + 1) * side].T

    def step(index, carry):
        taken = index - begin + used
        buffer = lax.rem(taken, buffers)

        @pl.when(taken >= buffers)
        def _():
            outer_wait(job, buffer, result, stage, sems)

        at = pl.ds(pl.multiple_of(index * step_width * side, step_width * side), step_width * side)
        values = right[:, at]
        for a in range(tall):
            tile = jnp.dot(turned[a], values, preferred_element_type=jnp.float32) * scale
            tile = tile.astype(jnp.bfloat16)
            for b in range(step_width):
                place = a * step_width + b
                stage[buffer, place] = tile[:, b * side : (b + 1) * side]
                slot = slots[0, a * wide + index * step_width + b]
                pltpu.make_async_copy(
                    stage.at[buffer, jnp.where(slot >= 0, place, zero_at)],
                    result.at[jnp.where(slot >= 0, slot, slot + region)],
                    sems.at[buffer],
                ).start()
        return carry

    lax.fori_loop(begin, end, step, 0)
    return used + end - begin


def outer_wait(job, buffer, result, stage, sems):
    taken = job[0] * job[2]
    pltpu.make_async_copy(
        stage.at[buffer, pl.ds(0, taken)], result.at[pl.ds(0, taken)], sems.at[buffer]
    ).wait()


def outer_kernel(jobs, carried, *refs):
    number = len(jobs)
    operands, rest = refs[: 3 * number], refs[3 * number + 1 + carried :]
    results, (turned, stage, sems) = rest[:number], rest[number + 1 :]
    side = stage.shape[-1]
    buffers = stage.shape[0]
    for buffer in range(buffers):
        stage[buffer, stage.shape[1] - 1] = jnp.zeros((side, side), stage.dtype)
    used = 0
    for index, (job, begin, end) in enumerate(jobs):
        slots, left, right = operands[3 * index : 3 * index + 3]
        used = outer_steps(job, begin, end, used, slots, left, right, results[index], turned, stage, sems)
        following = jobs[index + 1][0] if index + 1 < number else None
        if following is None or following[0] * following[2] != job[0] * job[2]:
            for taken in range(max(0, used - buffers), used):
                outer_wait(job, taken % buffers, results[index], stage, sems)
            used = 0


def outer_job(left, right, side):
    tall, wide = left.shape[1] // side, right.shape[1] // side
    return tall, wide, next(size for size in (4, 3, 2, 1) if wide % size == 0)


def outer_product(work, side, passed, carried, name):
    jobs = [one[:3] for one in work]
    operands = [value for one in work for value in one[3:]]
    shapes = [jax.ShapeDtypeStruct((job[0] * job[1], side, side), jnp.bfloat16) for job, _, _ in jobs]
    tallest = max(job[0] for job, _, _ in jobs)
    most = max(job[0] * job[2] for job, _, _ in jobs)
    extra = [] if carried is None else [carried]
    alias = {len(operands): len(jobs)}
    if carried is not None:
        alias[len(operands) + 1] = len(jobs) - 1
    return pl.pallas_call(
        functools.partial(outer_kernel, jobs, len(extra)),
        out_shape=(*shapes, jax.ShapeDtypeStruct(passed.shape, passed.dtype)),
        in_specs=[SMEM, VMEM, VMEM] * len(jobs) + [ANY] + [HBM] * len(extra),
        out_specs=(HBM,) * len(jobs) + (ANY,),
        scratch_shapes=[
            pltpu.VMEM((tallest, side, operands[1].shape[0]), jnp.bfloat16),
            pltpu.VMEM((2, most + 1, side, side), jnp.bfloat16),
            pltpu.SemaphoreType.DMA((2,)),
        ],
        input_output_aliases=alias,
        compiler_params=pltpu.CompilerParams(vmem_limit_bytes=16 << 20),
        cost_estimate=pl.CostEstimate(
            flops=0,
            bytes_accessed=sum(2 * job[0] * job[2] * (end - begin) for job, begin, end in jobs) * side * side,
            transcendentals=0,
        ),
        name=name,
    )(*operands, passed, *extra)


def exchange(values, away, devices):
    return lax.ppermute(values, "dp", [(i, i ^ away) for i in range(devices)])


def gather(values, devices):
    if devices != 8:
        return lax.all_gather(values, "dp", axis=0, tiled=True)
    near = jnp.concatenate([values, exchange(values, 4, devices)], axis=0)
    rest = [exchange(near, away, devices) for away in (2, 3, 1)]
    return jnp.concatenate([near] + rest, axis=0)


def near_sum(parts, devices):
    total = parts[0].astype(jnp.float32)
    for part, away in zip(parts[1:], (2, 3, 1)):
        total = total + exchange(part, away, devices).astype(jnp.float32)
    return total


def far_sum(total, rows, devices):
    mine = [total[0:rows], total[2 * rows : 3 * rows]]
    theirs = jnp.concatenate([total[rows : 2 * rows], total[3 * rows :]], axis=0).astype(jnp.bfloat16)
    far = exchange(theirs, 4, devices).astype(jnp.float32)
    return [(mine[i] + far[i * rows : (i + 1) * rows]).astype(jnp.bfloat16) for i in range(2)]


def full_sum(both, rows):
    results = []
    for first in (0, rows):
        whole = jnp.concatenate([part[first : first + rows] for part in both], axis=0)
        summed = lax.psum_scatter(whole.astype(jnp.float32), "dp", scatter_dimension=0, tiled=True)
        results.append(summed.astype(jnp.bfloat16))
    return results


def swap(values, devices):
    return lax.ppermute(values, "mp", [(i, (i + 1) % devices) for i in range(devices)])


def shards(
    tokens,
    cotangent,
    inward_blocks,
    inward_rows,
    inward_cols,
    inward_count,
    outward_blocks,
    outward_rows,
    outward_cols,
    outward_count,
):
    side = inward_blocks.shape[-1]
    region = inward_blocks.shape[2]
    row_blocks = tokens.shape[1] // side
    col_blocks = region // row_blocks
    n_dp = lax.axis_size("dp")
    n_mp = lax.axis_size("mp")
    pieces = 4 if n_dp == 8 else n_dp
    inward = inward_blocks.reshape(region, side, side)
    outward = outward_blocks.reshape(region, side, side)
    in_slots, out_slots = slot_maps(
        (inward_rows, inward_cols, outward_rows, outward_cols),
        (inward_count, outward_count),
        col_blocks,
        row_blocks,
    )
    all_tokens = gather(tokens, n_dp)
    all_grads = gather(cotangent, n_dp)
    hid_own, hid_sent = first_product(
        in_slots, all_tokens, inward, in_slots, row_blocks, col_blocks, False, True, "hidden"
    )
    hid_other = swap(hid_sent, n_mp)
    act_own, act_sent = first_product(
        out_slots, all_grads, outward, hid_own, row_blocks, col_blocks, True, False, "grad_act"
    )
    act_other = swap(act_sent, n_mp)
    activated, out_parts = output_product(
        out_slots, hid_own, hid_other, outward, act_own, col_blocks, row_blocks, pieces
    )
    grad_hidden, both = gradient_product(
        in_slots, (hid_own, hid_other, act_own, act_other), inward, out_parts, col_blocks, row_blocks
    )
    rows = tokens.shape[0]
    out_job = outer_job(activated, all_grads, side)
    in_job = outer_job(all_tokens, grad_hidden, side)
    in_steps = in_job[1] // in_job[2]
    begun = in_steps // 3
    work = [(out_job, 0, out_job[1] // out_job[2], out_slots, activated, all_grads)]
    if begun:
        work.append((in_job, 0, begun, in_slots, all_tokens, grad_hidden))
    grad_outward, *started, own = outer_product(work, side, both[0], None, "outward")
    both = [own, *both[1:]]
    nearly = near_sum(both, n_dp) if n_dp == 8 else own
    work = [(in_job, begun, in_steps, in_slots, all_tokens, grad_hidden)]
    grad_inward, _ = outer_product(work, side, nearly[0:8, 0:128], started[0] if begun else None, "inward")
    out_tokens, grad_tokens = far_sum(nearly, rows, n_dp) if n_dp == 8 else full_sum(both, rows)
    return (
        out_tokens,
        grad_tokens,
        grad_inward.reshape(inward_blocks.shape),
        grad_outward.reshape(outward_blocks.shape),
    )


def solution(mesh):
    in_specs = (
        P(("sweep", "dp"), "mp"),
        P(("sweep", "dp"), "mp"),
        P(("sweep", "mp"), "dp", None, None, None),
        P(("sweep", "mp"), "dp", None),
        P(("sweep", "mp"), "dp", None),
        P(("sweep", "mp"), "dp"),
        P(("sweep", "dp"), "mp", None, None, None),
        P(("sweep", "dp"), "mp", None),
        P(("sweep", "dp"), "mp", None),
        P(("sweep", "dp"), "mp"),
    )
    out_specs = (
        P(("sweep", "dp"), "mp"),
        P(("sweep", "dp"), "mp"),
        P(("sweep", "mp"), "dp", None, None, None),
        P(("sweep", "dp"), "mp", None, None, None),
    )
    return jax.shard_map(shards, mesh=mesh, in_specs=in_specs, out_specs=out_specs, check_vma=False)
```

```python
import functools

import jax
import jax.numpy as jnp
from jax import lax
from jax.experimental import pallas as pl
from jax.experimental.pallas import tpu as pltpu
from jax.sharding import PartitionSpec as P

root_half = 0.7071067811865476
inv_root_tau = 0.3989422804014327

SMEM = pl.BlockSpec(memory_space=pltpu.SMEM)
VMEM = pl.BlockSpec(memory_space=pltpu.VMEM)
ANY = pl.BlockSpec(memory_space=pl.ANY)
HBM = pl.BlockSpec(memory_space=pltpu.HBM)
GRANT = 4 << 20


def gelu_curve(values):
    return 0.5 * values * (1.0 + lax.erf(values * root_half))


def gelu_slope(values):
    return (
        0.5 * (1.0 + lax.erf(values * root_half))
        + values * jnp.exp(-0.5 * values * values) * inv_root_tau
    )


def slots_kernel(widths, *refs):
    far, counts, slots, near, (spread_out, sems) = refs[:4], refs[4:6], refs[7:9], refs[9:13], refs[13:]
    copies = [pltpu.make_async_copy(*ends, sems.at[index]) for index, ends in enumerate(zip(far, near))]
    for copy in copies:
        copy.start()
    for copy in copies:
        copy.wait()
    region = near[0].shape[-1]
    lanes = spread_out.shape[-1]
    side = 128
    down = lax.broadcasted_iota(jnp.int32, (side, side), 0)
    along = lax.broadcasted_iota(jnp.int32, (side, side), 1)
    positions = lax.broadcasted_iota(jnp.int32, (side, lanes), 1)
    for which, width in enumerate(widths):
        rows, cols, kept = near[2 * which], near[2 * which + 1], counts[which]
        spread_out[...] = jnp.full(spread_out.shape, -1, jnp.int32)
        spread_out[0:1, 0:region] = rows[0] * width + cols[0]
        total = jnp.zeros((1, lanes), jnp.int32)
        for start in range(0, lanes, side):
            there = jnp.broadcast_to(spread_out[0:1, start : start + side], (side, side))
            column = jnp.sum(jnp.where(down == along, there, 0), axis=1, keepdims=True)
            slot = lax.broadcasted_iota(jnp.int32, (side, lanes), 0) + start
            code = jnp.where(slot < kept[0, 0], slot, slot - region)
            total += jnp.sum(jnp.where(column == positions, code, 0), axis=0, keepdims=True)
        slots[which][...] = total[:, 0:region]


def slot_maps(places, counts, earlier, in_width, out_width):
    region = places[0].shape[-1]
    lanes = -(-region // 128) * 128
    shape = jax.ShapeDtypeStruct((1, region), jnp.int32)
    near = [pltpu.VMEM(place.shape, place.dtype) for place in places]
    return pl.pallas_call(
        functools.partial(slots_kernel, (in_width, out_width)),
        out_shape=(shape, shape),
        in_specs=[HBM] * 4 + [SMEM] * 2 + [ANY],
        out_specs=(VMEM, VMEM),
        scratch_shapes=near + [pltpu.VMEM((8, lanes), jnp.int32), pltpu.SemaphoreType.DMA((4,))],
        compiler_params=pltpu.CompilerParams(vmem_limit_bytes=GRANT),
        cost_estimate=pl.CostEstimate(flops=0, bytes_accessed=4 << 20, transcendentals=0),
        name="slot_maps",
    )(*[in_hbm(place) for place in places], *counts, earlier)


def pair(count):
    return 2 if count % 2 == 0 else 1


def product(lhs_ref, block, side, depth, deep, wide, across):
    total = None
    for k0 in range(0, depth, deep):
        if across:
            tile = jnp.concatenate(
                [jnp.concatenate([block(k0 + k, n) for k in range(deep)], axis=1) for n in range(wide)],
                axis=0,
            )
            dims = (((1,), (1,)), ((), ()))
        else:
            tile = jnp.concatenate(
                [jnp.concatenate([block(k0 + k, n) for n in range(wide)], axis=1) for k in range(deep)],
                axis=0,
            )
            dims = (((1,), (0,)), ((), ()))
        lhs = lhs_ref[:, k0 * side : (k0 + deep) * side]
        part = lax.dot_general(lhs, tile, dims, preferred_element_type=jnp.float32)
        total = part if total is None else total + part
    return total


def multiply(lhs_ref, blocks_ref, slots_ref, depth, width, across, store):
    side = blocks_ref.shape[-1]
    deep, wide = pair(depth), pair(width)

    def column(step, carry):
        n0 = step * wide

        def block(k, n):
            slot = slots_ref[0, (n0 + n) * depth + k if across else k * width + n0 + n]
            found = blocks_ref[jnp.maximum(slot, 0)]
            return jnp.where(slot >= 0, found, jnp.zeros_like(found))

        total = product(lhs_ref, block, side, depth, deep, wide, across)
        store(pl.multiple_of(n0 * side, wide * side), wide * side, total)
        return carry

    steps = width // wide
    lax.fori_loop(0, steps, column, 0, unroll=pair(steps))


def stream(lhs_ref, blocks_ref, slots_ref, depth, width, across, store, fetched, sems):
    side = blocks_ref.shape[-1]
    deep = pair(depth)
    buffers = fetched.shape[0]
    wide = fetched.shape[1] // depth
    steps = width // wide

    def slot(step, k, n):
        column = step * wide + n
        return slots_ref[0, column * depth + k if across else k * width + column]

    def fetch(step, buffer):
        for n in range(wide):
            for k in range(depth):
                code = slot(step, k, n)
                source = jnp.where(code >= 0, code, code + blocks_ref.shape[0])
                pltpu.make_async_copy(
                    blocks_ref.at[source], fetched.at[buffer, k * wide + n], sems.at[buffer]
                ).start()

    def column(step, buffer):
        pltpu.make_async_copy(
            blocks_ref.at[pl.ds(0, depth * wide)], fetched.at[buffer], sems.at[buffer]
        ).wait()

        def block(k, n):
            found = fetched[buffer, k * wide + n]
            return jnp.where(slot(step, k, n) >= 0, found, jnp.zeros_like(found))

        store(
            pl.multiple_of(step * wide * side, wide * side),
            wide * side,
            product(lhs_ref, block, side, depth, deep, wide, across),
        )

    ahead = buffers - 1
    for step in range(ahead):
        fetch(step, step)

    def both(step, carry):
        fetch(step + ahead, lax.rem(step + ahead, buffers))
        column(step, lax.rem(step, buffers))
        return carry

    lax.fori_loop(0, steps - ahead, both, 0)
    for step in range(steps - ahead, steps):
        column(step, step % buffers)


def first_kernel(depth, width, across, pieces, slots, *refs):
    parts, (blocks, earlier, whole, own, sent, *fetch) = refs[:pieces], refs[pieces:]
    rows = whole.shape[0] // pieces
    for index, part in enumerate(parts):
        whole[index * rows : (index + 1) * rows] = part[...]

    def store(start, size, total):
        own[:, pl.ds(start, size)] = total
        sent[:, pl.ds(start, size)] = total.astype(jnp.bfloat16)

    run = stream if fetch else multiply
    run(whole, blocks, slots, depth, width, across, store, *fetch)


def first_product(slots, parts, blocks, earlier, depth, width, across, streamed, name):
    side = blocks.shape[-1]
    count = sum(part.shape[0] for part in parts)
    shape = (count, width * side)
    scratch, grant = [], GRANT
    if streamed:
        wide = next(size for size in (4, 3, 2, 1) if width % size == 0)
        buffers = min(3, width // wide)
        scratch = [
            pltpu.VMEM((buffers, depth * wide, side, side), blocks.dtype),
            pltpu.SemaphoreType.DMA((buffers,)),
        ]
        grant = 16 << 20
    return pl.pallas_call(
        functools.partial(first_kernel, depth, width, across, len(parts)),
        out_shape=(
            jax.ShapeDtypeStruct((count, depth * side), jnp.bfloat16),
            jax.ShapeDtypeStruct(shape, jnp.float32),
            jax.ShapeDtypeStruct(shape, jnp.bfloat16),
        ),
        in_specs=[SMEM] + [VMEM] * len(parts) + [HBM if streamed else VMEM, ANY],
        out_specs=(VMEM, VMEM, VMEM),
        scratch_shapes=scratch,
        compiler_params=pltpu.CompilerParams(vmem_limit_bytes=grant),
        cost_estimate=pl.CostEstimate(
            flops=2 * count * depth * width * side * side, bytes_accessed=2 * blocks.size, transcendentals=0
        ),
        name=name,
    )(slots, *parts, in_hbm(blocks) if streamed else in_vmem(blocks), earlier)


def in_hbm(values):
    return pltpu.with_memory_space_constraint(values, pltpu.HBM)


def in_vmem(blocks):
    return pltpu.with_memory_space_constraint(blocks, pltpu.VMEM)


def spread(parts, rows, start_row):
    def store(start, size, total):
        rounded = total.astype(jnp.bfloat16)
        for index, part in enumerate(parts):
            part[start_row : start_row + rows, pl.ds(start, size)] = rounded[index * rows : (index + 1) * rows]

    return store


def output_kernel(depth, width, rows, slots, own, other, blocks, earlier, activated, *parts):
    side = blocks.shape[-1]

    def activate(step, carry):
        at = pl.ds(pl.multiple_of(step * side, side), side)
        hidden = own[:, at] + other[:, at].astype(jnp.float32)
        activated[:, at] = gelu_curve(hidden).astype(jnp.bfloat16)
        return carry

    lax.fori_loop(0, depth, activate, 0)
    multiply(activated, blocks, slots, depth, width, False, spread(parts, rows, 0))


def output_product(slots, own, other, blocks, earlier, depth, width, pieces):
    count = own.shape[0]
    side = blocks.shape[-1]
    rows = count // pieces
    shapes = [jax.ShapeDtypeStruct((count, depth * side), jnp.bfloat16)]
    shapes += [jax.ShapeDtypeStruct((rows, width * side), jnp.bfloat16)] * pieces
    activated, *parts = pl.pallas_call(
        functools.partial(output_kernel, depth, width, rows),
        out_shape=tuple(shapes),
        in_specs=[SMEM, VMEM, VMEM, VMEM, ANY],
        out_specs=(VMEM,) * len(shapes),
        compiler_params=pltpu.CompilerParams(vmem_limit_bytes=GRANT),
        cost_estimate=pl.CostEstimate(
            flops=2 * count * depth * width * side * side, bytes_accessed=2 * blocks.size, transcendentals=0
        ),
        name="output",
    )(slots, own, other, in_vmem(blocks), earlier)
    return activated, parts


def gradient_kernel(depth, width, rows, pieces, slots, hid_own, hid_other, act_own, act_other, blocks, *refs):
    out_parts, (grad_hidden, *both) = refs[:pieces], refs[pieces:]
    side = blocks.shape[-1]

    def activate(step, carry):
        at = pl.ds(pl.multiple_of(step * side, side), side)
        hidden = hid_own[:, at] + hid_other[:, at].astype(jnp.float32)
        grad_act = act_own[:, at] + act_other[:, at].astype(jnp.float32)
        grad_hidden[:, at] = (grad_act * gelu_slope(hidden)).astype(jnp.bfloat16)
        return carry

    lax.fori_loop(0, depth, activate, 0)
    for part, out_part in zip(both, out_parts):
        part[:rows] = out_part[...]
    multiply(grad_hidden, blocks, slots, depth, width, True, spread(both, rows, rows))


def gradient_product(slots, values, blocks, out_parts, depth, width):
    count = values[0].shape[0]
    side = blocks.shape[-1]
    pieces = len(out_parts)
    rows = count // pieces
    shapes = [jax.ShapeDtypeStruct((count, depth * side), jnp.bfloat16)]
    shapes += [jax.ShapeDtypeStruct((2 * rows, width * side), jnp.bfloat16)] * pieces
    grad_hidden, *both = pl.pallas_call(
        functools.partial(gradient_kernel, depth, width, rows, pieces),
        out_shape=tuple(shapes),
        in_specs=[SMEM] + [VMEM] * (5 + pieces),
        out_specs=(VMEM,) * len(shapes),
        compiler_params=pltpu.CompilerParams(vmem_limit_bytes=GRANT),
        cost_estimate=pl.CostEstimate(
            flops=2 * count * depth * width * side * side, bytes_accessed=2 * blocks.size, transcendentals=0
        ),
        name="grad_tokens",
    )(slots, *values, in_vmem(blocks), *out_parts)
    return grad_hidden, both


def outer_steps(job, begin, end, used, slots, left, right, result, turned, stage, sems):
    tall, wide, step_width = job
    count = left.shape[0]
    side = result.shape[-1]
    region = tall * wide
    buffers = stage.shape[0]
    scale = float(count) ** (-0.5)
    zero_at = stage.shape[1] - 1
    for a in range(tall):
        turned[a] = left[:, a * side : (a + 1) * side].T

    def step(index, carry):
        taken = index - begin + used
        buffer = lax.rem(taken, buffers)

        @pl.when(taken >= buffers)
        def _():
            outer_wait(job, buffer, result, stage, sems)

        at = pl.ds(pl.multiple_of(index * step_width * side, step_width * side), step_width * side)
        values = right[:, at]
        for a in range(tall):
            tile = jnp.dot(turned[a], values, preferred_element_type=jnp.float32) * scale
            tile = tile.astype(jnp.bfloat16)
            for b in range(step_width):
                place = a * step_width + b
                stage[buffer, place] = tile[:, b * side : (b + 1) * side]
                slot = slots[0, a * wide + index * step_width + b]
                pltpu.make_async_copy(
                    stage.at[buffer, jnp.where(slot >= 0, place, zero_at)],
                    result.at[jnp.where(slot >= 0, slot, slot + region)],
                    sems.at[buffer],
                ).start()
        return carry

    lax.fori_loop(begin, end, step, 0)
    return used + end - begin


def outer_wait(job, buffer, result, stage, sems):
    taken = job[0] * job[2]
    pltpu.make_async_copy(
        stage.at[buffer, pl.ds(0, taken)], result.at[pl.ds(0, taken)], sems.at[buffer]
    ).wait()


def outer_kernel(jobs, carried, *refs):
    number = len(jobs)
    operands, rest = refs[: 3 * number], refs[3 * number + 1 + carried :]
    results, (turned, stage, sems) = rest[:number], rest[number + 1 :]
    side = stage.shape[-1]
    buffers = stage.shape[0]
    for buffer in range(buffers):
        stage[buffer, stage.shape[1] - 1] = jnp.zeros((side, side), stage.dtype)
    used = 0
    for index, (job, begin, end) in enumerate(jobs):
        slots, left, right = operands[3 * index : 3 * index + 3]
        used = outer_steps(job, begin, end, used, slots, left, right, results[index], turned, stage, sems)
        following = jobs[index + 1][0] if index + 1 < number else None
        if following is None or following[0] * following[2] != job[0] * job[2]:
            for taken in range(max(0, used - buffers), used):
                outer_wait(job, taken % buffers, results[index], stage, sems)
            used = 0


def outer_job(left, right, side):
    tall, wide = left.shape[1] // side, right.shape[1] // side
    return tall, wide, next(size for size in (4, 3, 2, 1) if wide % size == 0)


def outer_product(work, side, passed, carried, name):
    jobs = [one[:3] for one in work]
    operands = [value for one in work for value in one[3:]]
    shapes = [jax.ShapeDtypeStruct((job[0] * job[1], side, side), jnp.bfloat16) for job, _, _ in jobs]
    tallest = max(job[0] for job, _, _ in jobs)
    most = max(job[0] * job[2] for job, _, _ in jobs)
    extra = [] if carried is None else [carried]
    alias = {len(operands): len(jobs)}
    if carried is not None:
        alias[len(operands) + 1] = len(jobs) - 1
    return pl.pallas_call(
        functools.partial(outer_kernel, jobs, len(extra)),
        out_shape=(*shapes, jax.ShapeDtypeStruct(passed.shape, passed.dtype)),
        in_specs=[SMEM, VMEM, VMEM] * len(jobs) + [ANY] + [HBM] * len(extra),
        out_specs=(HBM,) * len(jobs) + (ANY,),
        scratch_shapes=[
            pltpu.VMEM((tallest, side, operands[1].shape[0]), jnp.bfloat16),
            pltpu.VMEM((2, most + 1, side, side), jnp.bfloat16),
            pltpu.SemaphoreType.DMA((2,)),
        ],
        input_output_aliases=alias,
        compiler_params=pltpu.CompilerParams(vmem_limit_bytes=16 << 20),
        cost_estimate=pl.CostEstimate(
            flops=0,
            bytes_accessed=sum(2 * job[0] * job[2] * (end - begin) for job, begin, end in jobs) * side * side,
            transcendentals=0,
        ),
        name=name,
    )(*operands, passed, *extra)


def exchange(values, away, devices):
    return lax.ppermute(values, "dp", [(i, i ^ away) for i in range(devices)])


def gather(values, devices):
    if devices != 8:
        return [lax.all_gather(values, "dp", axis=0, tiled=True)]
    near = jnp.concatenate([values, exchange(values, 4, devices)], axis=0)
    return [near] + [exchange(near, away, devices) for away in (2, 3, 1)]


def near_sum(parts, devices):
    total = parts[0].astype(jnp.float32)
    for part, away in zip(parts[1:], (2, 3, 1)):
        total = total + exchange(part, away, devices).astype(jnp.float32)
    return total


def far_sum(total, rows, devices):
    mine = [total[0:rows], total[2 * rows : 3 * rows]]
    theirs = jnp.concatenate([total[rows : 2 * rows], total[3 * rows :]], axis=0).astype(jnp.bfloat16)
    far = exchange(theirs, 4, devices).astype(jnp.float32)
    return [(mine[i] + far[i * rows : (i + 1) * rows]).astype(jnp.bfloat16) for i in range(2)]


def full_sum(both, rows):
    results = []
    for first in (0, rows):
        whole = jnp.concatenate([part[first : first + rows] for part in both], axis=0)
        summed = lax.psum_scatter(whole.astype(jnp.float32), "dp", scatter_dimension=0, tiled=True)
        results.append(summed.astype(jnp.bfloat16))
    return results


def swap(values, devices):
    return lax.ppermute(values, "mp", [(i, (i + 1) % devices) for i in range(devices)])


def shards(
    tokens,
    cotangent,
    inward_blocks,
    inward_rows,
    inward_cols,
    inward_count,
    outward_blocks,
    outward_rows,
    outward_cols,
    outward_count,
):
    side = inward_blocks.shape[-1]
    region = inward_blocks.shape[2]
    row_blocks = tokens.shape[1] // side
    col_blocks = region // row_blocks
    n_dp = lax.axis_size("dp")
    n_mp = lax.axis_size("mp")
    pieces = 4 if n_dp == 8 else n_dp
    inward = inward_blocks.reshape(region, side, side)
    outward = outward_blocks.reshape(region, side, side)
    token_parts = gather(tokens, n_dp)
    grad_parts = gather(cotangent, n_dp)
    in_slots, out_slots = slot_maps(
        (inward_rows, inward_cols, outward_rows, outward_cols),
        (inward_count, outward_count),
        token_parts[0],
        col_blocks,
        row_blocks,
    )
    all_tokens, hid_own, hid_sent = first_product(
        in_slots, token_parts, inward, in_slots, row_blocks, col_blocks, False, True, "hidden"
    )
    hid_other = swap(hid_sent, n_mp)
    all_grads, act_own, act_sent = first_product(
        out_slots, grad_parts, outward, hid_own, row_blocks, col_blocks, True, False, "grad_act"
    )
    act_other = swap(act_sent, n_mp)
    activated, out_parts = output_product(
        out_slots, hid_own, hid_other, outward, act_own, col_blocks, row_blocks, pieces
    )
    grad_hidden, both = gradient_product(
        in_slots, (hid_own, hid_other, act_own, act_other), inward, out_parts, col_blocks, row_blocks
    )
    rows = tokens.shape[0]
    out_job = outer_job(activated, all_grads, side)
    in_job = outer_job(all_tokens, grad_hidden, side)
    in_steps = in_job[1] // in_job[2]
    begun = in_steps // 3
    work = [(out_job, 0, out_job[1] // out_job[2], out_slots, activated, all_grads)]
    if begun:
        work.append((in_job, 0, begun, in_slots, all_tokens, grad_hidden))
    grad_outward, *started, own = outer_product(work, side, both[0], None, "outward")
    both = [own, *both[1:]]
    nearly = near_sum(both, n_dp) if n_dp == 8 else own
    work = [(in_job, begun, in_steps, in_slots, all_tokens, grad_hidden)]
    grad_inward, _ = outer_product(work, side, nearly[0:8, 0:128], started[0] if begun else None, "inward")
    out_tokens, grad_tokens = far_sum(nearly, rows, n_dp) if n_dp == 8 else full_sum(both, rows)
    return (
        out_tokens,
        grad_tokens,
        grad_inward.reshape(inward_blocks.shape),
        grad_outward.reshape(outward_blocks.shape),
    )


def solution(mesh):
    in_specs = (
        P(("sweep", "dp"), "mp"),
        P(("sweep", "dp"), "mp"),
        P(("sweep", "mp"), "dp", None, None, None),
        P(("sweep", "mp"), "dp", None),
        P(("sweep", "mp"), "dp", None),
        P(("sweep", "mp"), "dp"),
        P(("sweep", "dp"), "mp", None, None, None),
        P(("sweep", "dp"), "mp", None),
        P(("sweep", "dp"), "mp", None),
        P(("sweep", "dp"), "mp"),
    )
    out_specs = (
        P(("sweep", "dp"), "mp"),
        P(("sweep", "dp"), "mp"),
        P(("sweep", "mp"), "dp", None, None, None),
        P(("sweep", "dp"), "mp", None, None, None),
    )
    return jax.shard_map(shards, mesh=mesh, in_specs=in_specs, out_specs=out_specs, check_vma=False)
```
